256 devices in a mesh: gx: 16 (over y, x), yz: 16 (over z, core).
Axes of the slice: x: 4, y: 4, z: 8, core: 2. Of those that a mesh axis runs over, the one named last changes fastest.
Arguments:
- tokens: bfloat16 [512, 9216], P(None, ('gx', 'yz')), may hold values from -6 to 6
- gate_weight: bfloat16 [9216, 36864], P('gx', 'yz'), may hold values from -0.0625 to 0.0625
- up_weight: bfloat16 [9216, 36864], P('gx', 'yz'), may hold values from -0.0625 to 0.0625
- down_weight: bfloat16 [36864, 9216], P('yz', 'gx'), may hold values from -0.03125 to 0.03125
- exponents_hidden: int32 [16, 576], P('gx', 'yz'), may hold values from -9 to -6
- exponents_output: int32 [16, 144], P('yz', 'gx'), may hold values from -9 to -6
Outputs:
- mixed: bfloat16 [512, 9216], P(None, ('gx', 'yz'))
- hidden: bfloat16 [512, 36864], P(None, ('yz', 'gx'))
The draws below stay inside these ranges and needn't reach their ends.
All inputs are finite; a program needn't handle non-finite values.
Results may differ from the reference program's by a relative error of at most 0.034.
Values may be sent and summed in bfloat16 or wider, within the bound.
A program may use at most 64 MiB of HBM per device.

```python
import jax
import jax.numpy as jnp
from jax import lax

D = 9216
FF = 36864
QB = 64
ROWS = 512
N_GX = 16
N_YZ = 16


def set_ends(values, own_key, least, largest):
    place = [jax.random.randint(jax.random.fold_in(own_key, axis), (), 0, length) for axis, length in enumerate(values.shape)]
    longest = values.shape.index(max(values.shape))
    neighbour = place[:longest] + [(place[longest] + 1) % values.shape[longest]] + place[longest + 1:]
    return values.at[tuple(place)].set(least).at[tuple(neighbour)].set(largest)


def shard_levels(key, dims, split, smallest, largest):
    def one(dim, parts):
        steps = jax.random.uniform(jax.random.fold_in(jax.random.fold_in(key, 6), dim), (parts,), jnp.float32, smallest / len(split), largest / len(split))
        return jnp.repeat(jnp.exp(steps), dims[dim] // parts).reshape((-1,) + (1,) * (len(dims) - dim - 1))

    gain = one(*split[0])
    for cut in split[1:]:
        gain = gain * one(*cut)
    return gain


def gaussian(own_key, shape, scale, limit, pieces=(), dtype=jnp.bfloat16):
    drawn = scale * jax.random.normal(own_key, shape, jnp.float32)
    if pieces:
        drawn = drawn * shard_levels(own_key, shape, pieces, -0.22, 0.18)
    return jnp.clip(drawn, -limit, limit).astype(dtype)


def setup_inputs(seed: int = 0) -> dict:
    keys = jax.random.split(jax.random.key(seed), 7)
    tokens = gaussian(keys[0], (ROWS, D), 1.0, 6.0, ((1, 256),))
    gate_weight = gaussian(keys[1], (D, FF), D ** -0.5, 0.0625, ((0, 16), (1, 16)))
    up_weight = gaussian(keys[2], (D, FF), D ** -0.5, 0.0625, ((0, 16), (1, 16)))
    down_weight = gaussian(keys[3], (FF, D), FF ** -0.5, 0.03125, ((0, 16), (1, 16)))
    exponents_hidden = set_ends(jax.random.randint(keys[4], (N_GX, FF // QB), -9, -5), jax.random.fold_in(keys[4], 1), -9, (-5) - 1).astype(jnp.int32)
    exponents_output = set_ends(jax.random.randint(keys[5], (N_YZ, D // QB), -9, -5), jax.random.fold_in(keys[5], 1), -9, (-5) - 1).astype(jnp.int32)
    return {"tokens": tokens, "gate_weight": gate_weight, "up_weight": up_weight, "down_weight": down_weight, "exponents_hidden": exponents_hidden, "exponents_output": exponents_output}


saturation = 127.0


def saturate(partial_value, exponents):
    scale = jnp.repeat(jnp.exp2(exponents.astype(jnp.float32)), partial_value.shape[-1] // exponents.shape[-1])
    return jnp.clip(partial_value / scale, -saturation, saturation) * scale


def settle(term):
    return lax.optimization_barrier(term.astype(jnp.bfloat16)).astype(jnp.float32)


def reference(tokens, gate_weight, up_weight, down_weight, exponents_hidden, exponents_output):
    group_feat = D // N_GX
    token_groups = tokens.reshape(ROWS, N_GX, group_feat).transpose(1, 0, 2)
    gate_groups = gate_weight.reshape(N_GX, group_feat, FF)
    up_groups = up_weight.reshape(N_GX, group_feat, FF)

    def first_step(carry, items):
        piece, gate_rows, up_rows, exponents = items
        gate_part = jnp.dot(piece, gate_rows, preferred_element_type=jnp.float32)
        up_part = jnp.dot(piece, up_rows, preferred_element_type=jnp.float32)
        return (carry[0] + settle(saturate(gate_part, exponents)), carry[1] + settle(saturate(up_part, exponents))), None

    start = jnp.zeros((ROWS, FF), jnp.float32)
    (gate_sum, up_sum), _ = lax.scan(first_step, (start, start), (token_groups, gate_groups, up_groups, exponents_hidden))
    hidden = (jax.nn.silu(gate_sum) * up_sum).astype(jnp.bfloat16)

    group_hid = FF // N_YZ
    hidden_groups = hidden.reshape(ROWS, N_YZ, group_hid).transpose(1, 0, 2)
    down_groups = down_weight.reshape(N_YZ, group_hid, D)

    def second_step(carry, items):
        piece, down_rows, exponents = items
        output_part = jnp.dot(piece, down_rows, preferred_element_type=jnp.float32)
        return carry + settle(saturate(output_part, exponents)), None

    total, _ = lax.scan(second_step, jnp.zeros((ROWS, D), jnp.float32), (hidden_groups, down_groups, exponents_output))
    return total.astype(jnp.bfloat16), hidden
```

```python
import functools

import jax
import jax.numpy as jnp
from jax import lax
from jax.experimental import pallas as pl
from jax.experimental.pallas import tpu as pltpu
from jax.sharding import PartitionSpec as P

saturation = 127.0
MESH = pl.DeviceIdType.MESH
f32 = jnp.float32
bf16 = jnp.bfloat16

ROWS = 512
K = 4
L = ROWS // K
FEAT = 576
HID = 2304
BLK = 144
OWN = 36
PAD = 48
QB = 64
NSEM = 64


def kernel(
    t_ref, gw_hbm, uw_hbm, dw_hbm, eh_ref, eo_ref,
    mixed_ref, hidden_ref,
    w_in, w_t, dw, tok, tok_f, tok_b,
    parts, r1a, r1b, s1, r2, hid,
    out_f, ob, obr, oz, ozr,
    local_sem, send_sem, recv_sem,
):
    gx = lax.axis_index("gx")
    yz = lax.axis_index("yz")
    x = lax.rem(gx, 4)
    y = lax.div(gx, 4)
    z = lax.div(yz, 2)
    c = lax.rem(yz, 2)
    gx_at = lambda yy, xx: (yy * 4 + xx, yz)
    at_x = lambda d: gx_at(y, lax.rem(x + d, 4))
    at_y = lambda d: gx_at(lax.rem(y + d, 4), x)
    at_z = lambda d: (gx, lax.rem(z + d, 8) * 2 + c)
    sibling = (gx, z * 2 + 1 - c)

    loads = [
        pltpu.make_async_copy(gw_hbm, w_in.at[0], local_sem.at[0]),
        pltpu.make_async_copy(uw_hbm, w_in.at[1], local_sem.at[1]),
        pltpu.make_async_copy(dw_hbm, dw, local_sem.at[2]),
    ]
    for load in loads:
        load.start()

    barrier = pltpu.get_barrier_semaphore()
    partners = [at_z(d) for d in range(1, 8)] + [sibling]
    partners += [at_x(d) for d in range(1, 4)] + [at_y(d) for d in range(1, 4)]
    for partner in partners:
        pl.semaphore_signal(barrier, inc=1, device_id=partner, device_id_type=MESH)

    for k in range(K):
        tok[k, c, z] = jnp.zeros((PAD, L), bf16)
        tok[k, c, z, 0:OWN, :] = t_ref[:, k * L:(k + 1) * L]
    pl.semaphore_wait(barrier, len(partners))

    sent = {}

    def send(k, i, src, dst, to):
        copy = pltpu.make_async_remote_copy(
            src_ref=src, dst_ref=dst, send_sem=send_sem.at[k, i], recv_sem=recv_sem.at[k, i],
            device_id=to, device_id_type=MESH,
        )
        copy.start()
        sent[k, i] = copy

    def arrived(k, i):
        sent[k, i].wait_recv()

    TOK, TOKC, R1A, R1B, R2, A1, A2, A2F, OC, OZ = 0, 7, 8, 12, 20, 26, 32, 40, 44, 45

    for k in range(K):
        for d in range(1, 8):
            send(k, TOK + d - 1, tok.at[k, c, z], tok.at[k, c, z], at_z(d))

    for m in range(2):
        loads[m].wait()

        @pl.loop(0, HID // 128)
        def _(j):
            cols = pl.ds(pl.multiple_of(j * 128, 128), 128)
            w_t[m, cols, :] = w_in[m, :, cols].T

    place = ((x, y), (y, x))
    first = (at_x, at_y)
    second = (at_y, at_x)

    def piece(k, m, dest, half):
        two = pl.ds(2 * half, 2)
        return parts.at[k, 0, two, dest] if m == 0 else parts.at[k, 1, dest, two]

    def tokens_stage(k):
        for d in range(1, 8):
            arrived(k, TOK + d - 1)
        send(k, TOKC, tok.at[k, c], tok.at[k, c], sibling)

    def first_stage(k):
        arrived(k, TOKC)
        for b in range(16):
            tok_f[b * OWN:(b + 1) * OWN, :] = tok[k, b % 2, b // 2, 0:OWN, :].astype(f32)
        tok_b[...] = tok_f[...].astype(bf16)

        for m in range(2):
            @pl.loop(0, 4)
            def _(j):
                rows = pl.ds(pl.multiple_of(j * FEAT, FEAT), FEAT)
                part = jnp.dot(w_t[m, rows, :], tok_b[...], preferred_element_type=f32)
                terms = []
                for b in range(FEAT // QB):
                    e = eh_ref[0, j * (FEAT // QB) + b]
                    most = jnp.left_shift(jnp.int32(1), e + 16).astype(f32) * (saturation * 2.0 ** -16)
                    terms.append(jnp.clip(part[b * QB:(b + 1) * QB], -most, most).astype(bf16))
                term = jnp.concatenate(terms, axis=0)
                parts[k, m, j] = term.reshape(4, BLK, L)

            p = place[m][0]
            right, left, opposite = lax.rem(p + 1, 4), lax.rem(p + 3, 4), lax.rem(p + 2, 4)
            send(k, R1A + 2 * m, piece(k, m, opposite, 0), r1a.at[k, m, 0], first[m](1))
            send(k, R1A + 2 * m + 1, piece(k, m, opposite, 1), r1a.at[k, m, 1], first[m](3))
            send(k, R1B + 4 * m, piece(k, m, right, 1), r1b.at[k, m, 0, 1], first[m](1))
            send(k, R1B + 4 * m + 1, piece(k, m, left, 0), r1b.at[k, m, 1, 0], first[m](3))

    def second_stage(k):
        for m in range(2):
            p = place[m][0]
            right, left = lax.rem(p + 1, 4), lax.rem(p + 3, 4)
            for half, dest, way in ((0, right, 1), (1, left, 3)):
                arrived(k, R1A + 2 * m + half)
                mine = piece(k, m, dest, half)
                mine[...] = (mine[...].astype(f32) + r1a[k, m, half].astype(f32)).astype(bf16)
                send(k, R1B + 4 * m + 2 + half, mine, r1b.at[k, m, half, half], first[m](way))

    def third_stage(k):
        for m in range(2):
            p, q = place[m]
            for i in range(4):
                arrived(k, R1B + 4 * m + i)
            for half in range(2):
                total = piece(k, m, p, half)[...].astype(f32)
                total += r1b[k, m, 0, half].astype(f32)
                total += r1b[k, m, 1, half].astype(f32)
                s1[k, m, 2 * half:2 * half + 2] = total.astype(bf16)
            for d in range(1, 4):
                send(k, R2 + 3 * m + d - 1, s1.at[k, m, lax.rem(q + d, 4)], r2.at[k, m, d - 1], second[m](d))

    def cut(k):
        low = 80 if k % 2 == 0 else 64
        return (pl.ds(0, low), pl.ds(low, BLK - low))

    def fourth_stage(k):
        sums = []
        for m in range(2):
            q = place[m][1]
            total = s1[k, m, q].astype(f32)
            for d in range(1, 4):
                arrived(k, R2 + 3 * m + d - 1)
                total += r2[k, m, d - 1].astype(f32)
            sums.append(total)
        gate_sum, up_sum = sums
        hidden = (gate_sum / (1.0 + jnp.exp(-gate_sum)) * up_sum).astype(bf16)
        hid[k, y, x] = hidden
        hidden_ref[:, k * L:(k + 1) * L] = hidden
        for h in range(2):
            own = hid.at[k, y, x, cut(k)[h]]
            for d in range(1, 4):
                send(k, A1 + 3 * h + d - 1, own, own, first[h](d))

    def line(k, h, at, half):
        two = pl.ds(2 * half, 2)
        return hid.at[k, at, two, cut(k)[h]] if h == 0 else hid.at[k, two, at, cut(k)[h]]

    def fifth_stage(k):
        for h in range(2):
            for d in range(1, 4):
                arrived(k, A1 + 3 * h + d - 1)
            q = place[h][1]
            for i, (half, way) in enumerate(((0, 1), (1, 3), (1, 1), (0, 3))):
                ref = line(k, h, q, half)
                send(k, A2 + 4 * h + i, ref, ref, second[h](way))

    def sixth_stage(k):
        for h in range(2):
            q = place[h][1]
            for half, way in ((0, 1), (1, 3)):
                arrived(k, A2 + 4 * h + half)
                ref = line(k, h, lax.rem(q + (3 if half == 0 else 1), 4), half)
                send(k, A2F + 2 * h + half, ref, ref, second[h](way))

    def seventh_stage(k):
        for h in range(2):
            arrived(k, A2 + 4 * h + 2)
            arrived(k, A2 + 4 * h + 3)
            arrived(k, A2F + 2 * h)
            arrived(k, A2F + 2 * h + 1)
        whole = hid[k].reshape(HID, L)

        @pl.loop(0, 3)
        def _(j):
            rows = pl.ds(pl.multiple_of(j * 192, 192), 192)
            part = jnp.dot(dw[rows, :], whole, preferred_element_type=f32)
            for b in range(3):
                e = eo_ref[0, j * 3 + b]
                most = jnp.left_shift(jnp.int32(1), e + 16).astype(f32) * (saturation * 2.0 ** -16)
                out_f[pl.ds(pl.multiple_of(j * 192 + b * QB, QB), QB), :] = jnp.clip(part[b * QB:(b + 1) * QB], -most, most)

        for b in range(16):
            ob[k, b % 2, b // 2, 0:OWN, :] = out_f[b * OWN:(b + 1) * OWN, :].astype(bf16)
        send(k, OC, ob.at[k, 1 - c], obr.at[k], sibling)

    def eighth_stage(k):
        arrived(k, OC)
        oz[k] = (ob[k, c].astype(f32) + obr[k].astype(f32)).astype(bf16)
        for d in range(1, 8):
            send(k, OZ + d - 1, oz.at[k, lax.rem(z + d, 8)], ozr.at[k, d - 1], at_z(d))

    def last_stage(k):
        total = oz[k, z].astype(f32)
        for d in range(1, 8):
            arrived(k, OZ + d - 1)
            total += ozr[k, d - 1].astype(f32)
        mixed_ref[:, k * L:(k + 1) * L] = total[0:OWN].astype(bf16)

    for k in range(K):
        for b in range(2):
            ob[k, b] = jnp.zeros((8, PAD, L), bf16)

    stages = (
        tokens_stage, first_stage, second_stage, third_stage, fourth_stage, fifth_stage,
        sixth_stage, seventh_stage, eighth_stage, last_stage,
    )
    for slot in range(len(stages) + K - 1):
        if slot == K:
            loads[2].wait()
        for k in range(K):
            s = slot - k
            if 0 <= s < len(stages):
                stages[s](k)

    for copy in sent.values():
        copy.wait_send()


def on_device(tokens, gate_weight, up_weight, down_weight, exponents_hidden, exponents_output):
    vmem = pl.BlockSpec(memory_space=pltpu.VMEM)
    smem = pl.BlockSpec(memory_space=pltpu.SMEM)
    hbm = pl.BlockSpec(memory_space=pl.ANY)
    mixed, hidden = pl.pallas_call(
        kernel,
        out_shape=(
            jax.ShapeDtypeStruct((OWN, ROWS), bf16),
            jax.ShapeDtypeStruct((BLK, ROWS), bf16),
        ),
        in_specs=[vmem, hbm, hbm, hbm, smem, smem],
        out_specs=(vmem, vmem),
        scratch_shapes=[
            pltpu.VMEM((2, FEAT, HID), bf16),
            pltpu.VMEM((2, HID, FEAT), bf16),
            pltpu.VMEM((FEAT, HID), bf16),
            pltpu.VMEM((K, 2, 8, PAD, L), bf16),
            pltpu.VMEM((FEAT, L), f32),
            pltpu.VMEM((FEAT, L), bf16),
            pltpu.VMEM((K, 2, 4, 4, BLK, L), bf16),
            pltpu.VMEM((K, 2, 2, 2, BLK, L), bf16),
            pltpu.VMEM((K, 2, 2, 2, 2, BLK, L), bf16),
            pltpu.VMEM((K, 2, 4, BLK, L), bf16),
            pltpu.VMEM((K, 2, 3, BLK, L), bf16),
            pltpu.VMEM((K, 4, 4, BLK, L), bf16),
            pltpu.VMEM((FEAT, L), f32),
            pltpu.VMEM((K, 2, 8, PAD, L), bf16),
            pltpu.VMEM((K, 8, PAD, L), bf16),
            pltpu.VMEM((K, 8, PAD, L), bf16),
            pltpu.VMEM((K, 7, PAD, L), bf16),
            pltpu.SemaphoreType.DMA((3,)),
            pltpu.SemaphoreType.DMA((K, NSEM)),
            pltpu.SemaphoreType.DMA((K, NSEM)),
        ],
        compiler_params=pltpu.CompilerParams(
            collective_id=0, has_side_effects=True, vmem_limit_bytes=56 << 20
        ),
    )(tokens.T, gate_weight, up_weight, down_weight.T, exponents_hidden, exponents_output)
    return mixed.T, hidden.T


def solution(mesh):
    placed = (
        P(None, ("gx", "yz")),
        P("gx", "yz"),
        P("gx", "yz"),
        P("yz", "gx"),
        P("gx", "yz"),
        P("yz", "gx"),
    )
    return jax.shard_map(
        on_device,
        mesh=mesh,
        in_specs=placed,
        out_specs=(P(None, ("gx", "yz")), P(None, ("yz", "gx"))),
        check_vma=False,
    )
```

```python
import functools

import jax
import jax.numpy as jnp
from jax import lax
from jax.experimental import pallas as pl
from jax.experimental.pallas import tpu as pltpu
from jax.sharding import PartitionSpec as P

saturation = 127.0
MESH = pl.DeviceIdType.MESH
f32 = jnp.float32
bf16 = jnp.bfloat16

ROWS = 512
K = 4
L = ROWS // K
FEAT = 576
HID = 2304
BLK = 144
OWN = 36
PAD = 48
QB = 64
NSEM = 64
ORDER = (
    ("TK", 0), ("T", 0), ("Mg", 0), ("Mu", 0), ("TK", 1), ("TK", 2), ("T", 1), ("Ag", 0),
    ("Mu", 1), ("Mg", 1), ("T", 2), ("Au", 0), ("TK", 3), ("Bg", 0), ("Mg", 2), ("Mu", 2),
    ("Bu", 0), ("T", 3), ("Au", 1), ("Mu", 3), ("Ag", 1), ("Mg", 3), ("Ag", 2), ("Bu", 1),
    ("Au", 2), ("Bg", 1), ("Au", 3), ("Ag", 3), ("C", 0), ("Bu", 2), ("Bg", 2), ("C", 1),
    ("Bg", 3), ("Bu", 3), ("D0", 0), ("D1", 0), ("C", 2), ("D1", 1), ("D0", 1), ("C", 3),
    ("E0", 0), ("E1", 0), ("E1", 1), ("D1", 2), ("E0", 1), ("D0", 2), ("D0", 3), ("D1", 3),
    ("F", 0), ("E1", 2), ("E0", 2), ("F", 1), ("E0", 3), ("G", 0), ("E1", 3), ("G", 1),
    ("F", 2), ("G", 2), ("F", 3), ("G", 3), ("H", 2), ("H", 0), ("H", 1), ("H", 3),
)
FAR_FIRST = (4, 3, 5, 2, 6, 1, 7)


def bound(exponent):
    return jnp.left_shift(jnp.int32(1), exponent + 16).astype(f32) * (saturation * 2.0 ** -16)


def kernel(
    t_hbm, gw_hbm, uw_hbm, dw_hbm, eh_ref, eo_ref,
    mixed_ref, hidden_ref,
    t_ref, most, w_in, w_t, dw, tok, tok_f, tok_b,
    parts, r1a, r1b, s1, r2, hid,
    out_f, ob, obr, oz, ozr,
    local_sem, send_sem, recv_sem,
):
    gx = lax.axis_index("gx")
    yz = lax.axis_index("yz")
    x = lax.rem(gx, 4)
    y = lax.div(gx, 4)
    z = lax.div(yz, 2)
    c = lax.rem(yz, 2)
    gx_at = lambda yy, xx: (yy * 4 + xx, yz)
    at_x = lambda d: gx_at(y, lax.rem(x + d, 4))
    at_y = lambda d: gx_at(lax.rem(y + d, 4), x)
    at_z = lambda d: (gx, lax.rem(z + d, 8) * 2 + c)
    sibling = (gx, z * 2 + 1 - c)

    load_t = pltpu.make_async_copy(t_hbm, t_ref, local_sem.at[3])
    load_t.start()
    loads = [
        pltpu.make_async_copy(gw_hbm, w_in.at[0], local_sem.at[0]),
        pltpu.make_async_copy(uw_hbm, w_in.at[1], local_sem.at[1]),
        pltpu.make_async_copy(dw_hbm, dw, local_sem.at[2]),
    ]
    for load in loads:
        load.start()

    barrier = pltpu.get_barrier_semaphore()
    partners = [at_z(d) for d in range(1, 8)] + [sibling]
    partners += [at_x(d) for d in range(1, 4)] + [at_y(d) for d in range(1, 4)]
    for partner in partners:
        pl.semaphore_signal(barrier, inc=1, device_id=partner, device_id_type=MESH)

    load_t.wait()
    for k in range(K):
        tok[k, c, z] = jnp.zeros((PAD, L), bf16)
        tok[k, c, z, 0:OWN, :] = t_ref[:, k * L:(k + 1) * L]
    pl.semaphore_wait(barrier, len(partners))

    sent = {}

    def send(k, i, src, dst, to):
        copy = pltpu.make_async_remote_copy(
            src_ref=src, dst_ref=dst, send_sem=send_sem.at[k, i], recv_sem=recv_sem.at[k, i],
            device_id=to, device_id_type=MESH,
        )
        copy.start()
        sent[k, i] = copy

    def arrived(k, i):
        sent[k, i].wait_recv()

    TOK, TOKC, R1A, R1B, R2, A1, A2, A2F, OC, OZ = 0, 7, 8, 12, 20, 26, 32, 40, 44, 45

    for k in range(K):
        for d in FAR_FIRST:
            send(k, TOK + d - 1, tok.at[k, c, z], tok.at[k, c, z], at_z(d))

    for b in range(HID // QB):
        most[b * QB:(b + 1) * QB, :] = jnp.full((QB, L), bound(eh_ref[0, b])).astype(bf16)

    for m in range(2):
        loads[m].wait()

        @pl.loop(0, HID // 128)
        def _(j):
            cols = pl.ds(pl.multiple_of(j * 128, 128), 128)
            w_t[m, cols, :] = w_in[m, :, cols].T

    place = ((x, y), (y, x))
    first = (at_x, at_y)
    second = (at_y, at_x)

    def piece(k, m, dest, half):
        two = pl.ds(2 * half, 2)
        return parts.at[k, 0, two, dest] if m == 0 else parts.at[k, 1, dest, two]

    def tokens_stage(k):
        for d in range(1, 8):
            arrived(k, TOK + d - 1)
        send(k, TOKC, tok.at[k, c], tok.at[k, c], sibling)

    def assemble(k):
        arrived(k, TOKC)
        for b in range(16):
            tok_f[b * OWN:(b + 1) * OWN, :] = tok[k, b % 2, b // 2, 0:OWN, :].astype(f32)
        tok_b[k] = tok_f[...].astype(bf16)

    def multiply(k, m):
        p = place[m][0]
        for d in (2, 1, 3, 0):
            dest = lax.rem(p + d, 4)
            blocks = [4 * i + dest if m == 0 else 4 * dest + i for i in range(4)]
            rows = [pl.ds(pl.multiple_of(b * BLK, BLK), BLK) for b in blocks]
            weight = jnp.concatenate([w_t[m, r, :] for r in rows], axis=0)
            part = jnp.dot(weight, tok_b[k], preferred_element_type=f32).astype(bf16)
            for i, r in enumerate(rows):
                term = jnp.clip(part[i * BLK:(i + 1) * BLK], -most[r, :], most[r, :])
                if m == 0:
                    parts[k, 0, i, dest] = term
                else:
                    parts[k, 1, dest, i] = term
            if d == 2:
                send(k, R1A + 2 * m, piece(k, m, dest, 0), r1a.at[k, m, 0], first[m](1))
                send(k, R1A + 2 * m + 1, piece(k, m, dest, 1), r1a.at[k, m, 1], first[m](3))
            elif d == 1:
                send(k, R1B + 4 * m, piece(k, m, dest, 1), r1b.at[k, m, 0, 1], first[m](1))
            elif d == 3:
                send(k, R1B + 4 * m + 1, piece(k, m, dest, 0), r1b.at[k, m, 1, 0], first[m](3))

    def middle(k, m):
        p = place[m][0]
        right, left = lax.rem(p + 1, 4), lax.rem(p + 3, 4)
        for half, dest, way in ((0, right, 1), (1, left, 3)):
            arrived(k, R1A + 2 * m + half)
            mine = piece(k, m, dest, half)
            mine[...] = (mine[...].astype(f32) + r1a[k, m, half].astype(f32)).astype(bf16)
            send(k, R1B + 4 * m + 2 + half, mine, r1b.at[k, m, half, half], first[m](way))

    def line_sum(k, m):
        p, q = place[m]
        for i in range(4):
            arrived(k, R1B + 4 * m + i)
        for half in range(2):
            total = piece(k, m, p, half)[...].astype(f32)
            total += r1b[k, m, 0, half].astype(f32)
            total += r1b[k, m, 1, half].astype(f32)
            s1[k, m, 2 * half:2 * half + 2] = total.astype(bf16)
        for d in range(1, 4):
            send(k, R2 + 3 * m + d - 1, s1.at[k, m, lax.rem(q + d, 4)], r2.at[k, m, d - 1], second[m](d))

    def cut(k):
        low = 80 if k % 2 == 0 else 64
        return (pl.ds(0, low), pl.ds(low, BLK - low))

    def gated(k):
        sums = []
        for m in range(2):
            q = place[m][1]
            total = s1[k, m, q].astype(f32)
            for d in range(1, 4):
                arrived(k, R2 + 3 * m + d - 1)
                total += r2[k, m, d - 1].astype(f32)
            sums.append(total)
        gate_sum, up_sum = sums
        hidden = (gate_sum / (1.0 + jnp.exp(-gate_sum)) * up_sum).astype(bf16)
        hid[k, y, x] = hidden
        hidden_ref[:, k * L:(k + 1) * L] = hidden
        for h in range(2):
            own = hid.at[k, y, x, cut(k)[h]]
            for d in range(1, 4):
                send(k, A1 + 3 * h + d - 1, own, own, first[h](d))

    def line(k, h, at, half):
        two = pl.ds(2 * half, 2)
        return hid.at[k, at, two, cut(k)[h]] if h == 0 else hid.at[k, two, at, cut(k)[h]]

    def spread(k, h):
        for d in range(1, 4):
            arrived(k, A1 + 3 * h + d - 1)
        q = place[h][1]
        for i, (half, way) in enumerate(((0, 1), (1, 3), (1, 1), (0, 3))):
            ref = line(k, h, q, half)
            send(k, A2 + 4 * h + i, ref, ref, second[h](way))

    def forward(k, h):
        q = place[h][1]
        for half, way in ((0, 1), (1, 3)):
            arrived(k, A2 + 4 * h + half)
            ref = line(k, h, lax.rem(q + (3 if half == 0 else 1), 4), half)
            send(k, A2F + 2 * h + half, ref, ref, second[h](way))

    def project(k):
        for h in range(2):
            arrived(k, A2 + 4 * h + 2)
            arrived(k, A2 + 4 * h + 3)
            arrived(k, A2F + 2 * h)
            arrived(k, A2F + 2 * h + 1)
        whole = hid[k].reshape(HID, L)

        @pl.loop(0, 3, unroll=3)
        def _(j):
            rows = pl.ds(pl.multiple_of(j * 192, 192), 192)
            part = jnp.dot(dw[rows, :], whole, preferred_element_type=f32)
            for b in range(3):
                limit = bound(eo_ref[0, j * 3 + b])
                out_f[pl.ds(pl.multiple_of(j * 192 + b * QB, QB), QB), :] = jnp.clip(part[b * QB:(b + 1) * QB], -limit, limit)

        for b in range(16):
            ob[k, b % 2, b // 2, 0:OWN, :] = out_f[b * OWN:(b + 1) * OWN, :].astype(bf16)
        send(k, OC, ob.at[k, 1 - c], obr.at[k], sibling)

    def pair_sum(k):
        arrived(k, OC)
        oz[k] = (ob[k, c].astype(f32) + obr[k].astype(f32)).astype(bf16)
        for d in FAR_FIRST:
            send(k, OZ + d - 1, oz.at[k, lax.rem(z + d, 8)], ozr.at[k, d - 1], at_z(d))

    def finish(k):
        total = oz[k, z].astype(f32)
        for d in range(1, 8):
            arrived(k, OZ + d - 1)
            total += ozr[k, d - 1].astype(f32)
        mixed_ref[:, k * L:(k + 1) * L] = total[0:OWN].astype(bf16)

    for k in range(K):
        for b in range(2):
            ob[k, b] = jnp.zeros((8, PAD, L), bf16)

    stages = {
        "TK": tokens_stage, "T": assemble,
        "Mg": lambda k: multiply(k, 0), "Mu": lambda k: multiply(k, 1),
        "Ag": lambda k: middle(k, 0), "Au": lambda k: middle(k, 1),
        "Bg": lambda k: line_sum(k, 0), "Bu": lambda k: line_sum(k, 1),
        "C": gated,
        "D0": lambda k: spread(k, 0), "D1": lambda k: spread(k, 1),
        "E0": lambda k: forward(k, 0), "E1": lambda k: forward(k, 1),
        "F": project, "G": pair_sum, "H": finish,
    }
    for stage, k in ORDER:
        if (stage, k) == ("F", 0):
            loads[2].wait()
        stages[stage](k)

    for copy in sent.values():
        copy.wait_send()


def on_device(tokens, gate_weight, up_weight, down_weight, exponents_hidden, exponents_output):
    smem = pl.BlockSpec(memory_space=pltpu.SMEM)
    hbm = pl.BlockSpec(memory_space=pl.ANY)
    mixed, hidden = pl.pallas_call(
        kernel,
        out_shape=(
            pltpu.VMEM((OWN, ROWS), bf16),
            pltpu.VMEM((BLK, ROWS), bf16),
        ),
        in_specs=[hbm, hbm, hbm, hbm, smem, smem],
        out_specs=(pl.BlockSpec(memory_space=pltpu.VMEM), pl.BlockSpec(memory_space=pltpu.VMEM)),
        scratch_shapes=[
            pltpu.VMEM((OWN, ROWS), bf16),
            pltpu.VMEM((HID, L), bf16),
            pltpu.VMEM((2, FEAT, HID), bf16),
            pltpu.VMEM((2, HID, FEAT), bf16),
            pltpu.VMEM((FEAT, HID), bf16),
            pltpu.VMEM((K, 2, 8, PAD, L), bf16),
            pltpu.VMEM((FEAT, L), f32),
            pltpu.VMEM((K, FEAT, L), bf16),
            pltpu.VMEM((K, 2, 4, 4, BLK, L), bf16),
            pltpu.VMEM((K, 2, 2, 2, BLK, L), bf16),
            pltpu.VMEM((K, 2, 2, 2, 2, BLK, L), bf16),
            pltpu.VMEM((K, 2, 4, BLK, L), bf16),
            pltpu.VMEM((K, 2, 3, BLK, L), bf16),
            pltpu.VMEM((K, 4, 4, BLK, L), bf16),
            pltpu.VMEM((FEAT, L), f32),
            pltpu.VMEM((K, 2, 8, PAD, L), bf16),
            pltpu.VMEM((K, 8, PAD, L), bf16),
            pltpu.VMEM((K, 8, PAD, L), bf16),
            pltpu.VMEM((K, 7, PAD, L), bf16),
            pltpu.SemaphoreType.DMA((4,)),
            pltpu.SemaphoreType.DMA((K, NSEM)),
            pltpu.SemaphoreType.DMA((K, NSEM)),
        ],
        compiler_params=pltpu.CompilerParams(
            collective_id=0, has_side_effects=True, vmem_limit_bytes=56 << 20
        ),
    )(tokens.T, gate_weight, up_weight, down_weight.T, exponents_hidden, exponents_output)
    return mixed.T, hidden.T


def solution(mesh):
    placed = (
        P(None, ("gx", "yz")),
        P("gx", "yz"),
        P("gx", "yz"),
        P("yz", "gx"),
        P("gx", "yz"),
        P("yz", "gx"),
    )
    return jax.shard_map(
        on_device,
        mesh=mesh,
        in_specs=placed,
        out_specs=(P(None, ("gx", "yz")), P(None, ("yz", "gx"))),
        check_vma=False,
    )
```

```python
import functools

import jax
import jax.numpy as jnp
from jax import lax
from jax.experimental import pallas as pl
from jax.experimental.pallas import tpu as pltpu
from jax.sharding import PartitionSpec as P

saturation = 127.0
MESH = pl.DeviceIdType.MESH
f32 = jnp.float32
bf16 = jnp.bfloat16

ROWS = 512
K = 4
L = ROWS // K
FEAT = 576
HID = 2304
BLK = 144
OWN = 36
PAD = 48
QB = 64
NSEM = 64
ORDER = (
    ("TK", 0), ("T", 0), ("Mg", 0), ("Mu", 0), ("TK", 1), ("TK", 2), ("T", 1), ("Ag", 0),
    ("Mu", 1), ("Mg", 1), ("T", 2), ("Au", 0), ("TK", 3), ("Bg", 0), ("Mg", 2), ("Mu", 2),
    ("Bu", 0), ("T", 3), ("Au", 1), ("Mu", 3), ("Ag", 1), ("Mg", 3), ("Ag", 2), ("Bu", 1),
    ("Au", 2), ("Bg", 1), ("Au", 3), ("Ag", 3), ("C", 0), ("Bu", 2), ("Bg", 2), ("C", 1),
    ("Bg", 3), ("Bu", 3), ("D0", 0), ("D1", 0), ("C", 2), ("D1", 1), ("D0", 1), ("C", 3),
    ("E0", 0), ("E1", 0), ("E1", 1), ("D1", 2), ("E0", 1), ("D0", 2), ("D0", 3), ("D1", 3),
    ("F", 0), ("E1", 2), ("E0", 2), ("F", 1), ("E0", 3), ("G", 0), ("E1", 3), ("G", 1),
    ("F", 2), ("G", 2), ("F", 3), ("G", 3), ("H", 2), ("H", 0), ("H", 1), ("H", 3),
)
FAR_FIRST = (4, 3, 5, 2, 6, 1, 7)


def bound(exponent):
    return jnp.left_shift(jnp.int32(1), exponent + 16).astype(f32) * (saturation * 2.0 ** -16)


def kernel(
    t_hbm, gw_hbm, uw_hbm, dw_hbm, eh_ref, eo_ref,
    mixed_ref, hidden_ref,
    t_ref, most, w_in, w_t, dw, tok, tok_f, tok_b,
    parts, r1a, r1b, s1, r2, hid,
    out_f, ob, obr, oz, ozr,
    local_sem, send_sem, recv_sem,
):
    gx = lax.axis_index("gx")
    yz = lax.axis_index("yz")
    x = lax.rem(gx, 4)
    y = lax.div(gx, 4)
    z = lax.div(yz, 2)
    c = lax.rem(yz, 2)
    gx_at = lambda yy, xx: (yy * 4 + xx, yz)
    at_x = lambda d: gx_at(y, lax.rem(x + d, 4))
    at_y = lambda d: gx_at(lax.rem(y + d, 4), x)
    at_z = lambda d: (gx, lax.rem(z + d, 8) * 2 + c)
    sibling = (gx, z * 2 + 1 - c)

    load_t = pltpu.make_async_copy(t_hbm, t_ref, local_sem.at[3])
    load_t.start()
    loads = [
        pltpu.make_async_copy(gw_hbm, w_in.at[0], local_sem.at[0]),
        pltpu.make_async_copy(uw_hbm, w_in.at[1], local_sem.at[1]),
        pltpu.make_async_copy(dw_hbm, dw, local_sem.at[2]),
    ]
    for load in loads:
        load.start()

    barrier = pltpu.get_barrier_semaphore()
    partners = [at_z(d) for d in range(1, 8)] + [sibling]
    partners += [at_x(d) for d in range(1, 4)] + [at_y(d) for d in range(1, 4)]
    for partner in partners:
        pl.semaphore_signal(barrier, inc=1, device_id=partner, device_id_type=MESH)

    load_t.wait()
    for k in range(K):
        tok[k, c, z] = jnp.zeros((PAD, L), bf16)
        tok[k, c, z, 0:OWN, :] = t_ref[:, k * L:(k + 1) * L]
    pl.semaphore_wait(barrier, len(partners))

    sent = {}

    def send(k, i, src, dst, to):
        copy = pltpu.make_async_remote_copy(
            src_ref=src, dst_ref=dst, send_sem=send_sem.at[k, i], recv_sem=recv_sem.at[k, i],
            device_id=to, device_id_type=MESH,
        )
        copy.start()
        sent[k, i] = copy

    def arrived(k, i):
        sent[k, i].wait_recv()

    TOK, TOKC, R1A, R1B, R2, A1, A2, A2F, OC, OZ = 0, 7, 8, 12, 20, 26, 32, 40, 44, 45

    for k in range(K):
        for d in FAR_FIRST:
            send(k, TOK + d - 1, tok.at[k, c, z], tok.at[k, c, z], at_z(d))

    for b in range(HID // QB):
        most[b * QB:(b + 1) * QB, :] = jnp.full((QB, L), bound(eh_ref[0, b])).astype(bf16)

    for m in range(2):
        loads[m].wait()

        @pl.loop(0, HID // 128)
        def _(j):
            cols = pl.ds(pl.multiple_of(j * 128, 128), 128)
            w_t[m, cols, :] = w_in[m, :, cols].T

    place = ((x, y), (y, x))
    first = (at_x, at_y)
    second = (at_y, at_x)

    def piece(k, m, dest, half):
        two = pl.ds(2 * half, 2)
        return parts.at[k, 0, two, dest] if m == 0 else parts.at[k, 1, dest, two]

    def tokens_stage(k):
        for d in range(1, 8):
            arrived(k, TOK + d - 1)
        send(k, TOKC, tok.at[k, c], tok.at[k, c], sibling)

    def assemble(k):
        arrived(k, TOKC)
        for b in range(16):
            tok_f[b * OWN:(b + 1) * OWN, :] = tok[k, b % 2, b // 2, 0:OWN, :].astype(f32)
        tok_b[k] = tok_f[...].astype(bf16)

    def multiply(k, m):
        p = place[m][0]
        for d in (2, 1, 3, 0):
            dest = lax.rem(p + d, 4)
            blocks = [4 * i + dest if m == 0 else 4 * dest + i for i in range(4)]
            rows = [pl.ds(pl.multiple_of(b * BLK, BLK), BLK) for b in blocks]
            weight = jnp.concatenate([w_t[m, r, :] for r in rows], axis=0)
            part = jnp.dot(weight, tok_b[k], preferred_element_type=f32).astype(bf16)
            for i, r in enumerate(rows):
                term = jnp.clip(part[i * BLK:(i + 1) * BLK], -most[r, :], most[r, :])
                if m == 0:
                    parts[k, 0, i, dest] = term
                else:
                    parts[k, 1, dest, i] = term
            if d == 2:
                send(k, R1A + 2 * m, piece(k, m, dest, 0), r1a.at[k, m, 0], first[m](1))
                send(k, R1A + 2 * m + 1, piece(k, m, dest, 1), r1a.at[k, m, 1], first[m](3))
            elif d == 1:
                send(k, R1B + 4 * m, piece(k, m, dest, 1), r1b.at[k, m, 0, 1], first[m](1))
            elif d == 3:
                send(k, R1B + 4 * m + 1, piece(k, m, dest, 0), r1b.at[k, m, 1, 0], first[m](3))

    def middle(k, m):
        p = place[m][0]
        right, left = lax.rem(p + 1, 4), lax.rem(p + 3, 4)
        for half, dest, way in ((0, right, 1), (1, left, 3)):
            arrived(k, R1A + 2 * m + half)
            mine = piece(k, m, dest, half)
            mine[...] = (mine[...].astype(f32) + r1a[k, m, half].astype(f32)).astype(bf16)
            send(k, R1B + 4 * m + 2 + half, mine, r1b.at[k, m, half, half], first[m](way))

    def line_sum(k, m):
        p, q = place[m]
        for i in range(4):
            arrived(k, R1B + 4 * m + i)
        for half in range(2):
            total = piece(k, m, p, half)[...].astype(f32)
            total += r1b[k, m, 0, half].astype(f32)
            total += r1b[k, m, 1, half].astype(f32)
            s1[k, m, 2 * half:2 * half + 2] = total.astype(bf16)
        for d in range(1, 4):
            send(k, R2 + 3 * m + d - 1, s1.at[k, m, lax.rem(q + d, 4)], r2.at[k, m, d - 1], second[m](d))

    def cut(k):
        low = 80 if k % 2 == 0 else 64
        return (pl.ds(0, low), pl.ds(low, BLK - low))

    def gated(k):
        sums = []
        for m in range(2):
            q = place[m][1]
            total = s1[k, m, q].astype(f32)
            for d in range(1, 4):
                arrived(k, R2 + 3 * m + d - 1)
                total += r2[k, m, d - 1].astype(f32)
            sums.append(total)
        gate_sum, up_sum = sums
        hidden = (gate_sum / (1.0 + jnp.exp(-gate_sum)) * up_sum).astype(bf16)
        hid[k, y, x] = hidden
        hidden_ref[:, k * L:(k + 1) * L] = hidden
        for h in range(2):
            own = hid.at[k, y, x, cut(k)[h]]
            for d in range(1, 4):
                send(k, A1 + 3 * h + d - 1, own, own, first[h](d))

    def line(k, h, at, half):
        two = pl.ds(2 * half, 2)
        return hid.at[k, at, two, cut(k)[h]] if h == 0 else hid.at[k, two, at, cut(k)[h]]

    def spread(k, h):
        for d in range(1, 4):
            arrived(k, A1 + 3 * h + d - 1)
        q = place[h][1]
        for i, (half, way) in enumerate(((0, 1), (1, 3), (1, 1), (0, 3))):
            ref = line(k, h, q, half)
            send(k, A2 + 4 * h + i, ref, ref, second[h](way))

    def forward(k, h):
        q = place[h][1]
        for half, way in ((0, 1), (1, 3)):
            arrived(k, A2 + 4 * h + half)
            ref = line(k, h, lax.rem(q + (3 if half == 0 else 1), 4), half)
            send(k, A2F + 2 * h + half, ref, ref, second[h](way))

    def project(k):
        for h in range(2):
            arrived(k, A2 + 4 * h + 2)
            arrived(k, A2 + 4 * h + 3)
            arrived(k, A2F + 2 * h)
            arrived(k, A2F + 2 * h + 1)
        whole = hid[k].reshape(HID, L)

        @pl.loop(0, 3, unroll=3)
        def _(j):
            rows = pl.ds(pl.multiple_of(j * 192, 192), 192)
            part = jnp.dot(dw[rows, :], whole, preferred_element_type=f32)
            for b in range(3):
                limit = bound(eo_ref[0, j * 3 + b])
                out_f[pl.ds(pl.multiple_of(j * 192 + b * QB, QB), QB), :] = jnp.clip(part[b * QB:(b + 1) * QB], -limit, limit)

        for b in range(16):
            ob[k, b % 2, b // 2, 0:OWN, :] = out_f[b * OWN:(b + 1) * OWN, :].astype(bf16)
        send(k, OC, ob.at[k, 1 - c], obr.at[k], sibling)

    def pair_sum(k):
        arrived(k, OC)
        oz[k] = (ob[k, c].astype(f32) + obr[k].astype(f32)).astype(bf16)
        for d in FAR_FIRST:
            send(k, OZ + d - 1, oz.at[k, lax.rem(z + d, 8)], ozr.at[k, d - 1], at_z(d))

    def finish(k):
        total = oz[k, z].astype(f32)
        for d in range(1, 8):
            arrived(k, OZ + d - 1)
            total += ozr[k, d - 1].astype(f32)
        mixed_ref[:, k * L:(k + 1) * L] = total[0:OWN].astype(bf16)

    for k in range(K):
        for b in range(2):
            ob[k, b] = jnp.zeros((8, PAD, L), bf16)

    stages = {
        "TK": tokens_stage, "T": assemble,
        "Mg": lambda k: multiply(k, 0), "Mu": lambda k: multiply(k, 1),
        "Ag": lambda k: middle(k, 0), "Au": lambda k: middle(k, 1),
        "Bg": lambda k: line_sum(k, 0), "Bu": lambda k: line_sum(k, 1),
        "C": gated,
        "D0": lambda k: spread(k, 0), "D1": lambda k: spread(k, 1),
        "E0": lambda k: forward(k, 0), "E1": lambda k: forward(k, 1),
        "F": project, "G": pair_sum, "H": finish,
    }
    settled = set()
    for stage, k in ORDER:
        if (stage, k) == ("F", 0):
            loads[2].wait()
        if stage == "H":
            for key, copy in sent.items():
                if key not in settled and (key[0] < K - 1 or key[1] < OZ):
                    copy.wait_send()
                    settled.add(key)
        stages[stage](k)

    for key, copy in sent.items():
        if key not in settled:
            copy.wait_send()


def on_device(tokens, gate_weight, up_weight, down_weight, exponents_hidden, exponents_output):
    smem = pl.BlockSpec(memory_space=pltpu.SMEM)
    hbm = pl.BlockSpec(memory_space=pl.ANY)
    mixed, hidden = pl.pallas_call(
        kernel,
        out_shape=(
            pltpu.VMEM((OWN, ROWS), bf16),
            pltpu.VMEM((BLK, ROWS), bf16),
        ),
        in_specs=[hbm, hbm, hbm, hbm, smem, smem],
        out_specs=(pl.BlockSpec(memory_space=pltpu.VMEM), pl.BlockSpec(memory_space=pltpu.VMEM)),
        scratch_shapes=[
            pltpu.VMEM((OWN, ROWS), bf16),
            pltpu.VMEM((HID, L), bf16),
            pltpu.VMEM((2, FEAT, HID), bf16),
            pltpu.VMEM((2, HID, FEAT), bf16),
            pltpu.VMEM((FEAT, HID), bf16),
            pltpu.VMEM((K, 2, 8, PAD, L), bf16),
            pltpu.VMEM((FEAT, L), f32),
            pltpu.VMEM((K, FEAT, L), bf16),
            pltpu.VMEM((K, 2, 4, 4, BLK, L), bf16),
            pltpu.VMEM((K, 2, 2, 2, BLK, L), bf16),
            pltpu.VMEM((K, 2, 2, 2, 2, BLK, L), bf16),
            pltpu.VMEM((K, 2, 4, BLK, L), bf16),
            pltpu.VMEM((K, 2, 3, BLK, L), bf16),
            pltpu.VMEM((K, 4, 4, BLK, L), bf16),
            pltpu.VMEM((FEAT, L), f32),
            pltpu.VMEM((K, 2, 8, PAD, L), bf16),
            pltpu.VMEM((K, 8, PAD, L), bf16),
            pltpu.VMEM((K, 8, PAD, L), bf16),
            pltpu.VMEM((K, 7, PAD, L), bf16),
            pltpu.SemaphoreType.DMA((4,)),
            pltpu.SemaphoreType.DMA((K, NSEM)),
            pltpu.SemaphoreType.DMA((K, NSEM)),
        ],
        compiler_params=pltpu.CompilerParams(
            collective_id=0, has_side_effects=True, vmem_limit_bytes=56 << 20
        ),
    )(tokens.T, gate_weight, up_weight, down_weight.T, exponents_hidden, exponents_output)
    return mixed.T, hidden.T


def solution(mesh):
    placed = (
        P(None, ("gx", "yz")),
        P("gx", "yz"),
        P("gx", "yz"),
        P("yz", "gx"),
        P("gx", "yz"),
        P("yz", "gx"),
    )
    return jax.shard_map(
        on_device,
        mesh=mesh,
        in_specs=placed,
        out_specs=(P(None, ("gx", "yz")), P(None, ("yz", "gx"))),
        check_vma=False,
    )
```

```python
import functools

import jax
import jax.numpy as jnp
from jax import lax
from jax.experimental import pallas as pl
from jax.experimental.pallas import tpu as pltpu
from jax.sharding import PartitionSpec as P

saturation = 127.0
MESH = pl.DeviceIdType.MESH
f32 = jnp.float32
bf16 = jnp.bfloat16

ROWS = 512
K = 4
L = ROWS // K
FEAT = 576
HID = 2304
BLK = 144
OWN = 36
PAD = 48
QB = 64
NSEM = 64
ORDER = (
    ("TK", 0), ("T", 0), ("Mg", 0), ("Mu", 0), ("TK", 1), ("TK", 2), ("T", 1), ("Ag", 0),
    ("Mu", 1), ("Mg", 1), ("T", 2), ("Au", 0), ("TK", 3), ("Bg", 0), ("Mg", 2), ("Mu", 2),
    ("Bu", 0), ("T", 3), ("Au", 1), ("Mu", 3), ("Ag", 1), ("Mg", 3), ("Ag", 2), ("Bu", 1),
    ("Au", 2), ("Bg", 1), ("Au", 3), ("Ag", 3), ("C", 0), ("Bu", 2), ("Bg", 2), ("C", 1),
    ("Bg", 3), ("Bu", 3), ("D0", 0), ("D1", 0), ("C", 2), ("D1", 1), ("D0", 1), ("C", 3),
    ("E0", 0), ("E1", 0), ("E1", 1), ("D1", 2), ("E0", 1), ("D0", 2), ("D0", 3), ("D1", 3),
    ("F", 0), ("E1", 2), ("E0", 2), ("F", 1), ("E0", 3), ("G", 0), ("E1", 3), ("G", 1),
    ("F", 2), ("G", 2), ("F", 3), ("G", 3), ("H", 2), ("H", 0), ("H", 1), ("H", 3),
)
FAR_FIRST = (4, 3, 5, 2, 6, 1, 7)


def bound(exponent):
    return jnp.left_shift(jnp.int32(1), exponent + 16).astype(f32) * (saturation * 2.0 ** -16)


def kernel(
    t_hbm, gw_hbm, uw_hbm, dw_hbm, eh_ref, eo_ref,
    mixed_ref, hidden_ref,
    t_ref, most, w_in, w_t, dw, tok, tok_f, tok_b,
    parts, r1a, r1b, s1, r2, hid,
    out_f, ob, obr, oz, ozr,
    local_sem, send_sem, recv_sem,
):
    gx = lax.axis_index("gx")
    yz = lax.axis_index("yz")
    x = lax.rem(gx, 4)
    y = lax.div(gx, 4)
    z = lax.div(yz, 2)
    c = lax.rem(yz, 2)
    gx_at = lambda yy, xx: (yy * 4 + xx, yz)
    at_x = lambda d: gx_at(y, lax.rem(x + d, 4))
    at_y = lambda d: gx_at(lax.rem(y + d, 4), x)
    at_z = lambda d: (gx, lax.rem(z + d, 8) * 2 + c)
    sibling = (gx, z * 2 + 1 - c)

    barrier = pltpu.get_barrier_semaphore()
    partners = [at_z(d) for d in range(1, 8)] + [sibling]
    partners += [at_x(d) for d in range(1, 4)] + [at_y(d) for d in range(1, 4)]
    for partner in partners:
        pl.semaphore_signal(barrier, inc=1, device_id=partner, device_id_type=MESH)

    load_t = pltpu.make_async_copy(t_hbm, t_ref, local_sem.at[3])
    load_t.start()
    loads = [
        pltpu.make_async_copy(gw_hbm, w_in.at[0], local_sem.at[0]),
        pltpu.make_async_copy(uw_hbm, w_in.at[1], local_sem.at[1]),
        pltpu.make_async_copy(dw_hbm, dw, local_sem.at[2]),
    ]
    for load in loads:
        load.start()

    load_t.wait()
    for k in range(K):
        tok[k, c, z] = jnp.zeros((PAD, L), bf16)
        tok[k, c, z, 0:OWN, :] = t_ref[:, k * L:(k + 1) * L]
    pl.semaphore_wait(barrier, len(partners))

    sent = {}

    def send(k, i, src, dst, to):
        copy = pltpu.make_async_remote_copy(
            src_ref=src, dst_ref=dst, send_sem=send_sem.at[k, i], recv_sem=recv_sem.at[k, i],
            device_id=to, device_id_type=MESH,
        )
        copy.start()
        sent[k, i] = copy

    def arrived(k, i):
        sent[k, i].wait_recv()

    TOK, TOKC, R1A, R1B, R2, A1, A2, A2F, OC, OZ = 0, 7, 8, 12, 20, 26, 32, 40, 44, 45

    for k in range(K):
        for d in FAR_FIRST:
            send(k, TOK + d - 1, tok.at[k, c, z], tok.at[k, c, z], at_z(d))

    for b in range(HID // QB):
        most[b * QB:(b + 1) * QB, :] = jnp.full((QB, L), bound(eh_ref[0, b])).astype(bf16)

    for m in range(2):
        loads[m].wait()

        @pl.loop(0, HID // 128)
        def _(j):
            cols = pl.ds(pl.multiple_of(j * 128, 128), 128)
            w_t[m, cols, :] = w_in[m, :, cols].T

    place = ((x, y), (y, x))
    first = (at_x, at_y)
    second = (at_y, at_x)

    def piece(k, m, dest, half):
        two = pl.ds(2 * half, 2)
        return parts.at[k, 0, two, dest] if m == 0 else parts.at[k, 1, dest, two]

    def tokens_stage(k):
        for d in range(1, 8):
            arrived(k, TOK + d - 1)
        send(k, TOKC, tok.at[k, c], tok.at[k, c], sibling)

    def assemble(k):
        arrived(k, TOKC)
        for b in range(16):
            tok_f[b * OWN:(b + 1) * OWN, :] = tok[k, b % 2, b // 2, 0:OWN, :].astype(f32)
        tok_b[k] = tok_f[...].astype(bf16)

    def multiply(k, m):
        p = place[m][0]
        for d in (2, 1, 3, 0):
            dest = lax.rem(p + d, 4)
            blocks = [4 * i + dest if m == 0 else 4 * dest + i for i in range(4)]
            rows = [pl.ds(pl.multiple_of(b * BLK, BLK), BLK) for b in blocks]
            weight = jnp.concatenate([w_t[m, r, :] for r in rows], axis=0)
            part = jnp.dot(weight, tok_b[k], preferred_element_type=f32).astype(bf16)
            for i, r in enumerate(rows):
                term = jnp.clip(part[i * BLK:(i + 1) * BLK], -most[r, :], most[r, :])
                if m == 0:
                    parts[k, 0, i, dest] = term
                else:
                    parts[k, 1, dest, i] = term
            if d == 2:
                send(k, R1A + 2 * m, piece(k, m, dest, 0), r1a.at[k, m, 0], first[m](1))
                send(k, R1A + 2 * m + 1, piece(k, m, dest, 1), r1a.at[k, m, 1], first[m](3))
            elif d == 1:
                send(k, R1B + 4 * m, piece(k, m, dest, 1), r1b.at[k, m, 0, 1], first[m](1))
            elif d == 3:
                send(k, R1B + 4 * m + 1, piece(k, m, dest, 0), r1b.at[k, m, 1, 0], first[m](3))

    def middle(k, m):
        p = place[m][0]
        right, left = lax.rem(p + 1, 4), lax.rem(p + 3, 4)
        for half, dest, way in ((0, right, 1), (1, left, 3)):
            arrived(k, R1A + 2 * m + half)
            mine = piece(k, m, dest, half)
            mine[...] = (mine[...].astype(f32) + r1a[k, m, half].astype(f32)).astype(bf16)
            send(k, R1B + 4 * m + 2 + half, mine, r1b.at[k, m, half, half], first[m](way))

    def line_sum(k, m):
        p, q = place[m]
        for i in range(4):
            arrived(k, R1B + 4 * m + i)
        for half in range(2):
            total = piece(k, m, p, half)[...].astype(f32)
            total += r1b[k, m, 0, half].astype(f32)
            total += r1b[k, m, 1, half].astype(f32)
            s1[k, m, 2 * half:2 * half + 2] = total.astype(bf16)
        for d in range(1, 4):
            send(k, R2 + 3 * m + d - 1, s1.at[k, m, lax.rem(q + d, 4)], r2.at[k, m, d - 1], second[m](d))

    def cut(k):
        low = 80 if k % 2 == 0 else 64
        return (pl.ds(0, low), pl.ds(low, BLK - low))

    def gated(k):
        sums = []
        for m in range(2):
            q = place[m][1]
            total = s1[k, m, q].astype(f32)
            for d in range(1, 4):
                arrived(k, R2 + 3 * m + d - 1)
                total += r2[k, m, d - 1].astype(f32)
            sums.append(total)
        gate_sum, up_sum = sums
        hidden = (gate_sum / (1.0 + jnp.exp(-gate_sum)) * up_sum).astype(bf16)
        hid[k, y, x] = hidden
        hidden_ref[:, k * L:(k + 1) * L] = hidden
        for h in range(2):
            own = hid.at[k, y, x, cut(k)[h]]
            for d in range(1, 4):
                send(k, A1 + 3 * h + d - 1, own, own, first[h](d))

    def line(k, h, at, half):
        two = pl.ds(2 * half, 2)
        return hid.at[k, at, two, cut(k)[h]] if h == 0 else hid.at[k, two, at, cut(k)[h]]

    def spread(k, h):
        for d in range(1, 4):
            arrived(k, A1 + 3 * h + d - 1)
        q = place[h][1]
        for i, (half, way) in enumerate(((0, 1), (1, 3), (1, 1), (0, 3))):
            ref = line(k, h, q, half)
            send(k, A2 + 4 * h + i, ref, ref, second[h](way))

    def forward(k, h):
        q = place[h][1]
        for half, way in ((0, 1), (1, 3)):
            arrived(k, A2 + 4 * h + half)
            ref = line(k, h, lax.rem(q + (3 if half == 0 else 1), 4), half)
            send(k, A2F + 2 * h + half, ref, ref, second[h](way))

    def project(k):
        for h in range(2):
            arrived(k, A2 + 4 * h + 2)
            arrived(k, A2 + 4 * h + 3)
            arrived(k, A2F + 2 * h)
            arrived(k, A2F + 2 * h + 1)
        whole = hid[k].reshape(HID, L)

        @pl.loop(0, 3, unroll=3)
        def _(j):
            rows = pl.ds(pl.multiple_of(j * 192, 192), 192)
            part = jnp.dot(dw[rows, :], whole, preferred_element_type=f32)
            for b in range(3):
                limit = bound(eo_ref[0, j * 3 + b])
                out_f[pl.ds(pl.multiple_of(j * 192 + b * QB, QB), QB), :] = jnp.clip(part[b * QB:(b + 1) * QB], -limit, limit)

        for b in range(16):
            ob[k, b % 2, b // 2, 0:OWN, :] = out_f[b * OWN:(b + 1) * OWN, :].astype(bf16)
        send(k, OC, ob.at[k, 1 - c], obr.at[k], sibling)

    def pair_sum(k):
        arrived(k, OC)
        for d in FAR_FIRST + (0,):
            to = lax.rem(z + d, 8)
            oz[k, to] = (ob[k, c, to].astype(f32) + obr[k, to].astype(f32)).astype(bf16)
            if d:
                send(k, OZ + d - 1, oz.at[k, to], ozr.at[k, d - 1], at_z(d))

    def finish(k):
        total = oz[k, z].astype(f32)
        for d in range(1, 8):
            arrived(k, OZ + d - 1)
            total += ozr[k, d - 1].astype(f32)
        mixed_ref[:, k * L:(k + 1) * L] = total[0:OWN].astype(bf16)

    for k in range(K):
        for b in range(2):
            ob[k, b] = jnp.zeros((8, PAD, L), bf16)

    stages = {
        "TK": tokens_stage, "T": assemble,
        "Mg": lambda k: multiply(k, 0), "Mu": lambda k: multiply(k, 1),
        "Ag": lambda k: middle(k, 0), "Au": lambda k: middle(k, 1),
        "Bg": lambda k: line_sum(k, 0), "Bu": lambda k: line_sum(k, 1),
        "C": gated,
        "D0": lambda k: spread(k, 0), "D1": lambda k: spread(k, 1),
        "E0": lambda k: forward(k, 0), "E1": lambda k: forward(k, 1),
        "F": project, "G": pair_sum, "H": finish,
    }
    settled = set()
    for stage, k in ORDER:
        if (stage, k) == ("F", 0):
            loads[2].wait()
        if stage == "H":
            for key, copy in sent.items():
                if key not in settled and (key[0] < K - 1 or key[1] < OZ):
                    copy.wait_send()
                    settled.add(key)
        stages[stage](k)

    for key, copy in sent.items():
        if key not in settled:
            copy.wait_send()


def on_device(tokens, gate_weight, up_weight, down_weight, exponents_hidden, exponents_output):
    smem = pl.BlockSpec(memory_space=pltpu.SMEM)
    hbm = pl.BlockSpec(memory_space=pl.ANY)
    mixed, hidden = pl.pallas_call(
        kernel,
        out_shape=(
            pltpu.VMEM((OWN, ROWS), bf16),
            pltpu.VMEM((BLK, ROWS), bf16),
        ),
        in_specs=[hbm, hbm, hbm, hbm, smem, smem],
        out_specs=(pl.BlockSpec(memory_space=pltpu.VMEM), pl.BlockSpec(memory_space=pltpu.VMEM)),
        scratch_shapes=[
            pltpu.VMEM((OWN, ROWS), bf16),
            pltpu.VMEM((HID, L), bf16),
            pltpu.VMEM((2, FEAT, HID), bf16),
            pltpu.VMEM((2, HID, FEAT), bf16),
            pltpu.VMEM((FEAT, HID), bf16),
            pltpu.VMEM((K, 2, 8, PAD, L), bf16),
            pltpu.VMEM((FEAT, L), f32),
            pltpu.VMEM((K, FEAT, L), bf16),
            pltpu.VMEM((K, 2, 4, 4, BLK, L), bf16),
            pltpu.VMEM((K, 2, 2, 2, BLK, L), bf16),
            pltpu.VMEM((K, 2, 2, 2, 2, BLK, L), bf16),
            pltpu.VMEM((K, 2, 4, BLK, L), bf16),
            pltpu.VMEM((K, 2, 3, BLK, L), bf16),
            pltpu.VMEM((K, 4, 4, BLK, L), bf16),
            pltpu.VMEM((FEAT, L), f32),
            pltpu.VMEM((K, 2, 8, PAD, L), bf16),
            pltpu.VMEM((K, 8, PAD, L), bf16),
            pltpu.VMEM((K, 8, PAD, L), bf16),
            pltpu.VMEM((K, 7, PAD, L), bf16),
            pltpu.SemaphoreType.DMA((4,)),
            pltpu.SemaphoreType.DMA((K, NSEM)),
            pltpu.SemaphoreType.DMA((K, NSEM)),
        ],
        compiler_params=pltpu.CompilerParams(
            collective_id=0, has_side_effects=True, vmem_limit_bytes=56 << 20
        ),
    )(tokens.T, gate_weight, up_weight, down_weight.T, exponents_hidden, exponents_output)
    return mixed.T, hidden.T


def solution(mesh):
    placed = (
        P(None, ("gx", "yz")),
        P("gx", "yz"),
        P("gx", "yz"),
        P("yz", "gx"),
        P("gx", "yz"),
        P("yz", "gx"),
    )
    return jax.shard_map(
        on_device,
        mesh=mesh,
        in_specs=placed,
        out_specs=(P(None, ("gx", "yz")), P(None, ("yz", "gx"))),
        check_vma=False,
    )
```
